1024 devices in a mesh: rep: 16 (over x, core), exp: 64 (over y, z).
Axes of the slice: x: 8, y: 8, z: 8, core: 2. Of those that a mesh axis runs over, the one named last changes fastest.
Arguments:
- prompt_state: bfloat16 [512, 16, 128, 128], P('exp', 'rep'), may hold values from -6 to 6
- prompt_conv: bfloat16 [512, 16, 3, 384], P('exp', 'rep'), may hold values from -6 to 6
- slot_prompt: int32 [8192], P(('rep', 'exp')), may hold values from 0 to 7, as said below
- projected: bfloat16 [8192, 4, 16, 384], P(('rep', 'exp')), may hold values from -6 to 6
- conv_weight: bfloat16 [16, 4, 384], replicated, may hold values from -3 to 3
- log_decay: float32 [8192, 4, 16], P(('rep', 'exp')), may hold values from -2.5 to -0.02
- write_rate: float32 [8192, 4, 16], P(('rep', 'exp')), may hold values from 0.05 to 0.95
- gate_in: bfloat16 [8192, 4, 2048], P(('rep', 'exp')), may hold values from -6 to 6
- layer_in: bfloat16 [8192, 4, 2048], P(('rep', 'exp')), may hold values from -3 to 3
- head_gain: float32 [128], replicated, may hold values from 0.1 to 1.9
- post_gain: float32 [2048], replicated, may hold values from 0.1 to 1.9
- expert_ids: int32 [8192, 4, 10], P(('rep', 'exp')), may hold values from 0 to 63, all different within a row; in each aligned block of 32 rows (0 to 31, 32 to 63, ..., all dimensions but the last counted through in order) at most 8 rows name the same one
- route_weight: float32 [8192, 4, 10], P(('rep', 'exp')), may hold values from 0.02 to 0.25
- w_gate_up: bfloat16 [64, 2048, 1024], P('exp'), may hold values from -0.125 to 0.125
- w_down: bfloat16 [64, 512, 2048], P('exp'), may hold values from -0.25 to 0.25
Outputs:
- layer_out: bfloat16 [8192, 4, 2048], P(('rep', 'exp'))
The draws below stay inside these ranges and needn't reach their ends.
Inputs may be any that keep to these rules, and one draw needn't show every extreme that they name: `slot_prompt`: in every sample group (the devices that share an index along exp) each of the group's 8 prompts is named by exactly 16 of the group's samples. `expert_ids`: the 32 rows of one device name no expert more than 8 times, a bound that some block reaches; a row names 10 different experts.
All inputs are finite; a program needn't handle non-finite values.
Results may differ from the reference program's by a relative error of at most 0.012.
Values may be sent and summed in bfloat16 or wider, within the bound.
A program may use at most 32 MiB of HBM per device.

```python
import math
import jax
import jax.numpy as jnp
import numpy as np
from jax import lax

D = 2048
H = 16
DK = 128
DV = 128
CH = 384
CONV = 4
FE = 512
STEPS = 4
SAMPLES = 16
S_DEV = 8
PG = 8
PROMPTS = 512
TOKENS = 8192
EXPERTS = 64
TOPK = 10
ROWS = 32
CAP = 8
N_REP = 16
N_EXP = 64


def draw_slot_prompt(key, part):
    key = jax.random.fold_in(key, 7)
    per_group = N_REP * S_DEV
    subkeys = jax.random.split(key, N_EXP)
    shuffled = jax.vmap(lambda subkey: jax.random.permutation(subkey, per_group))(subkeys)
    prompt_of = (shuffled // SAMPLES).astype(jnp.int32)
    arranged = jnp.transpose(prompt_of.reshape(N_EXP, N_REP, S_DEV), (1, 0, 2)).reshape(-1)
    return arranged.astype(jnp.int32)


def block_levels(rng, dims, cuts, low, largest):
    def one(dim, blocks):
        heights = jax.random.uniform(jax.random.fold_in(jax.random.fold_in(rng, 6), dim), (blocks,), jnp.float32, low / len(cuts), largest / len(cuts))
        return jnp.repeat(jnp.exp(heights), dims[dim] // blocks).reshape((-1,) + (1,) * (len(dims) - dim - 1))

    loudness = one(*cuts[0])
    for cut in cuts[1:]:
        loudness = loudness * one(*cut)
    return loudness


def shared_out(rng, own, number, rows, count, top, reach, lean):
    ranking = jax.random.permutation(rng, count)
    heavy_load, common = shares(count, rows * top, reach, lean, True), shares(count, rows * top, reach, lean, False)
    places = jnp.arange(count)

    def named(sizes, rotation):
        used = int((sizes > 0).sum())
        fixed = max(1, used // 4)
        shifted = fixed + (places - fixed + rotation * (used - fixed)) % max(1, count - fixed)
        return jnp.zeros((count,), jnp.int32).at[ranking[jnp.where(places < fixed, places, shifted)]].set(jnp.asarray(sizes, jnp.int32))

    sizes = jnp.where(number % 4 == 0, named(heavy_load, number // 4), named(common, number - number // 4 - 1))
    mixed = jax.random.permutation(jax.random.fold_in(own, 3), count)
    source_of, taker = mixed[0:count // 2 * 2:2], mixed[1:count // 2 * 2:2]
    margin = jnp.minimum(sizes[source_of] - 1, reach - sizes[taker]) // 2
    margin = jnp.where((source_of == ranking[0]) | (taker == ranking[0]) | (sizes[taker] == 0), 0, jnp.maximum(margin, 0))
    shifted = jax.random.randint(jax.random.fold_in(own, 4), (count // 2,), 0, 1 << 20) % (margin + 1)
    sizes = sizes.at[source_of].add(-shifted).at[taker].add(shifted)
    labels = jnp.searchsorted(jnp.cumsum(sizes), jnp.arange(rows * top), side="right").astype(jnp.int32)
    listing = labels.reshape(top, rows).T
    listing = listing[jax.random.permutation(jax.random.fold_in(own, 1), rows)]
    rotation = jax.random.randint(jax.random.fold_in(own, 2), (rows, 1), 0, top)
    return jnp.take_along_axis(listing, (jnp.arange(top)[None, :] + rotation) % top, axis=1)


def shares(count, total, bound, slope, full):
    portions = [(1 << 20) // math.isqrt(grade ** slope) + 1 for grade in range(1, count + 1)]
    largest = bound if full else min(bound, max(-(-total // count), total * portions[0] // sum(portions)))
    least = 1 if total - largest >= count - 1 else 0
    counts, surplus = [largest] + [least] * (count - 1), total - largest - least * (count - 1)
    while surplus > 0:
        free = [i for i in range(1, count) if counts[i] < largest] or [i for i in range(1, count) if counts[i] < bound]
        mass, budget = sum([portions[i] for i in free]), surplus
        for i in free:
            addition = min(bound - counts[i], max(1, budget * portions[i] // mass), surplus)
            counts[i] = counts[i] + addition
            surplus = surplus - addition
    return np.array(counts)


def noise(own_key, shape, width, reach, pieces=(), kind=jnp.bfloat16):
    values = width * jax.random.normal(own_key, shape, jnp.float32)
    if pieces:
        values = values * block_levels(own_key, shape, pieces, -0.22, 0.18)
    return jnp.clip(values, -reach, reach).astype(kind)


def setup_inputs(seed: int = 0) -> dict:
    key_list = jax.random.split(jax.random.key(seed), 16)
    prompt_state = noise(key_list[0], (PROMPTS, H, DK, DV), 1.0, 6.0, ((0, 64), (1, 16)))
    prompt_conv = noise(key_list[1], (PROMPTS, H, CONV - 1, CH), 1.0, 6.0, ((0, 64), (1, 16)))
    slot_prompt = draw_slot_prompt(jax.random.fold_in(key_list[15], 71), 0)
    projected = noise(key_list[3], (TOKENS, STEPS, H, CH), 1.0, 6.0, ((0, 1024),))
    conv_weight = noise(key_list[4], (H, CONV, CH), 0.5, 3.0)
    log_decay = jnp.clip(-2.5 + 2.48 * jax.random.uniform(key_list[5], (TOKENS, STEPS, H), jnp.float32) ** block_levels(key_list[5], (TOKENS, STEPS, H), ((0, 1024),), -0.2, 0.2), -2.5, -0.02)
    write_rate = jnp.clip(0.05 + 0.9 * jax.random.uniform(key_list[6], (TOKENS, STEPS, H), jnp.float32) ** block_levels(key_list[6], (TOKENS, STEPS, H), ((0, 1024),), -0.2, 0.2), 0.05, 0.95)
    gate_in = noise(key_list[7], (TOKENS, STEPS, D), 1.0, 6.0, ((0, 1024),))
    layer_in = noise(key_list[8], (TOKENS, STEPS, D), 0.5, 3.0, ((0, 1024),))
    head_gain = jnp.clip(1.0 + 0.18 * jax.random.normal(key_list[9], (DV,), jnp.float32), 0.1, 1.9)
    post_gain = jnp.clip(1.0 + 0.18 * jax.random.normal(key_list[10], (D,), jnp.float32), 0.1, 1.9)
    expert_ids_keys = jax.random.split(jax.random.fold_in(key_list[11], 1), TOKENS * STEPS // ROWS)
    expert_ids_turns = jax.random.permutation(jax.random.fold_in(key_list[11], 3), TOKENS * STEPS // ROWS)
    expert_ids = jax.vmap(lambda own, number: shared_out(jax.random.fold_in(key_list[11], 2), own, number, ROWS, EXPERTS, TOPK, CAP, 2))(expert_ids_keys, expert_ids_turns).reshape((TOKENS, STEPS, TOPK))
    route_weight = jnp.clip(0.02 + 0.23 * jax.random.uniform(key_list[12], (TOKENS, STEPS, TOPK), jnp.float32) ** block_levels(key_list[12], (TOKENS, STEPS, TOPK), ((0, 1024),), -0.2, 0.2), 0.02, 0.25)
    w_gate_up = noise(key_list[13], (EXPERTS, D, 2 * FE), D ** -0.5, 0.125, ((0, 64),))
    w_down = noise(key_list[14], (EXPERTS, FE, D), FE ** -0.5, 0.25, ((0, 64),))
    return {"prompt_state": prompt_state, "prompt_conv": prompt_conv, "slot_prompt": slot_prompt, "projected": projected, "conv_weight": conv_weight, "log_decay": log_decay, "write_rate": write_rate, "gate_in": gate_in, "layer_in": layer_in, "head_gain": head_gain, "post_gain": post_gain, "expert_ids": expert_ids, "route_weight": route_weight, "w_gate_up": w_gate_up, "w_down": w_down}


EPSILON = 1e-06
HIGHEST = lax.Precision.HIGHEST

def swish(inputs):
    return inputs * jax.nn.sigmoid(inputs)

def conv_features(projected, conv_window, conv_weight):
    history = jnp.concatenate([jnp.transpose(conv_window, (0, 2, 1, 3)), projected], axis=1).astype(jnp.float32)
    taps_all = conv_weight.astype(jnp.float32)
    summed = jnp.zeros(projected.shape, jnp.float32)
    for tap_index in range(CONV):
        summed = summed + history[:, tap_index:tap_index + STEPS] * taps_all[:, tap_index]
    active = swish(summed)
    queries = active[..., :DK]
    keys_part = active[..., DK:2 * DK]
    values_part = active[..., 2 * DK:]
    queries = queries / jnp.sqrt(lax.optimization_barrier(jnp.sum(queries * queries, axis=-1, keepdims=True)) + EPSILON) * DK ** (-0.5)
    keys_part = keys_part / jnp.sqrt(lax.optimization_barrier(jnp.sum(keys_part * keys_part, axis=-1, keepdims=True)) + EPSILON)
    return (queries.astype(jnp.bfloat16), keys_part.astype(jnp.bfloat16), values_part.astype(jnp.bfloat16))

def mix_heads(read_all, gate_in, layer_in, head_gain, post_gain):
    normed = read_all / jnp.sqrt(lax.optimization_barrier(jnp.mean(read_all * read_all, axis=-1, keepdims=True)) + EPSILON) * head_gain
    flat_heads = normed.reshape(normed.shape[0], normed.shape[1], -1)
    residual = layer_in.astype(jnp.float32) + flat_heads * swish(gate_in.astype(jnp.float32))
    scaled = residual / jnp.sqrt(lax.optimization_barrier(jnp.mean(residual * residual, axis=-1, keepdims=True)) + EPSILON) * post_gain
    return (residual, scaled.astype(jnp.bfloat16))

def reference(prompt_state, prompt_conv, slot_prompt, projected, conv_weight, log_decay, write_rate, gate_in, layer_in, head_gain, post_gain, expert_ids, route_weight, w_gate_up, w_down):
    devices_n = N_REP * N_EXP
    token_index = jnp.arange(TOKENS, dtype=jnp.int32)
    group_index = token_index // S_DEV % N_EXP
    prompt_row = (group_index * PG + slot_prompt).astype(jnp.int32)
    block_rows = N_EXP * S_DEV

    def to_blocks(array_in):
        return array_in.reshape((N_REP, block_rows) + array_in.shape[1:])

    def one_block(block_args):
        block_prompts, proj_block, decay_block, rate_block = block_args
        state_now = prompt_state[block_prompts].astype(jnp.float32)
        queries, keys_part, values_part = conv_features(proj_block, prompt_conv[block_prompts], conv_weight)
        queries_f = queries.astype(jnp.float32)
        keys_f = keys_part.astype(jnp.float32)
        values_f = values_part.astype(jnp.float32)
        reads_list = []
        for position in range(STEPS):
            alpha_now = jnp.exp(decay_block[:, position])[:, :, None, None]
            state_now = alpha_now * state_now
            key_now = keys_f[:, position]
            recalled = jnp.einsum('bhd,bhde->bhe', key_now, state_now, precision=HIGHEST)
            written = rate_block[:, position][:, :, None] * (values_f[:, position] - recalled)
            state_now = state_now + key_now[:, :, :, None] * written[:, :, None, :]
            reads_list.append(jnp.einsum('bhd,bhde->bhe', queries_f[:, position], state_now, precision=HIGHEST))
        return jnp.stack(reads_list, axis=1)
    read_all = lax.map(one_block, (to_blocks(prompt_row), to_blocks(projected), to_blocks(log_decay), to_blocks(write_rate)))
    read_all = read_all.reshape(TOKENS, STEPS, H, DV)
    residual, normed_in = mix_heads(read_all, gate_in, layer_in, head_gain, post_gain)
    rows_all = normed_in.reshape(devices_n, ROWS, D)
    chosen = expert_ids.reshape(devices_n, ROWS * TOPK)
    entry_order = jnp.arange(ROWS * TOPK, dtype=jnp.int32)
    earlier = (chosen[:, :, None] == chosen[:, None, :]) & (entry_order[None, None, :] < entry_order[None, :, None])
    slot_index = lax.optimization_barrier(jnp.sum(earlier.astype(jnp.int32), axis=2)).astype(jnp.int32)
    target = (chosen * CAP + slot_index).astype(jnp.int32)
    device_index = jnp.arange(devices_n, dtype=jnp.int32)
    slot_table = jnp.full((devices_n, EXPERTS * CAP), ROWS, jnp.int32)
    slot_table = slot_table.at[device_index[:, None], target].set(jnp.broadcast_to((entry_order // TOPK).astype(jnp.int32), target.shape))
    per_expert = jnp.transpose(slot_table.reshape(devices_n, EXPERTS, CAP), (1, 0, 2))
    padded_rows = jnp.concatenate([rows_all, jnp.zeros((devices_n, 1, D), jnp.bfloat16)], axis=1)

    def one_expert(operands):
        picked_rows, gate_up, down_proj = operands
        arrived = padded_rows[device_index[:, None], picked_rows].reshape(-1, D)
        both_parts = jnp.dot(arrived, gate_up, preferred_element_type=jnp.float32)
        hidden = (swish(both_parts[:, :FE]) * both_parts[:, FE:]).astype(jnp.bfloat16)
        return jnp.dot(hidden, down_proj, preferred_element_type=jnp.float32).astype(jnp.bfloat16)
    expert_out = lax.map(one_expert, (per_expert, w_gate_up, w_down)).reshape(-1, D)
    combined = residual.reshape(devices_n, ROWS, D)
    chosen_rows = expert_ids.reshape(devices_n, ROWS, TOPK)
    slots_rows = slot_index.reshape(devices_n, ROWS, TOPK)
    weights_rows = route_weight.reshape(devices_n, ROWS, TOPK)
    for rank_index in range(TOPK):
        flat_index = ((chosen_rows[:, :, rank_index] * devices_n + device_index[:, None]) * CAP + slots_rows[:, :, rank_index]).astype(jnp.int32)
        combined = combined + weights_rows[:, :, rank_index, None] * expert_out[flat_index].astype(jnp.float32)
    return combined.reshape(TOKENS, STEPS, D).astype(jnp.bfloat16)
```

```python
import jax
import jax.numpy as jnp
from jax import lax
from jax.experimental import pallas as pl
from jax.experimental.pallas import tpu as pltpu
from jax.sharding import PartitionSpec as P

MESH = pl.DeviceIdType.MESH
F32 = jnp.float32
BF16 = jnp.bfloat16

DK = 128
CH = 384
CONV = 4
FE = 512
STEPS = 4
HEADS = 16
D = 2048
HALF = 1024
RING = 8
S_DEV = 8
PG = 8
ROWS = 32
CAP = 8
TOPK = 10
EPSILON = 1e-06
VMEM_BYTES = 56 << 20

OFFS = (0, 1, 7, 2, 6, 3, 5, 4)
BACK = tuple(OFFS.index((RING - o) % RING) for o in OFFS)
FAR_FIRST = tuple(range(RING - 1, 0, -1))


def place():
    rep = lax.axis_index("rep")
    exp = lax.axis_index("exp")
    return rep // 2, lax.rem(rep, 2), exp // RING, lax.rem(exp, RING)


def swish(inputs):
    return inputs * jax.nn.sigmoid(inputs)


def iota(shape, dim):
    return lax.broadcasted_iota(jnp.int32, shape, dim)


def mixer_kernel(
    px,
    aux,
    state,
    conv,
    taps,
    head_gain,
    gate_in,
    layer_in,
    post_gain,
    residual,
    normed_in,
    got_px,
    got_aux,
    states,
    reads,
    got_reads,
    send_px,
    recv_px,
    send_aux,
    recv_aux,
    send_reads,
    recv_reads,
):
    x, c, _, _ = place()
    me = x * 2 + c
    exp = lax.axis_index("exp")

    def peer(q, core):
        odd = lax.rem(q, 2)
        offset = odd * ((q + 1) // 2) + (1 - odd) * lax.rem(RING - q // 2, RING)
        return lax.rem(x + offset, RING) * 2 + lax.rem(c + core, 2)

    pairs = [(q, core) for q in range(RING - 1, -1, -1) for core in range(2) if (q, core) != (0, 0)]
    barrier = pltpu.get_barrier_semaphore()
    for q, core in pairs:
        pl.semaphore_signal(barrier, inc=1, device_id=(peer(q, core), exp), device_id_type=MESH)
    got_px[pl.ds(me, 1)] = px[pl.ds(me, 1)]
    got_aux[pl.ds(me, 1)] = aux[pl.ds(me, 1)]
    for p in range(PG):
        states[:, p * DK : (p + 1) * DK] = state[p]
    pl.semaphore_wait(barrier, len(pairs))

    def copy_px(there, slot):
        return pltpu.make_async_remote_copy(
            src_ref=px.at[there],
            dst_ref=got_px.at[slot],
            send_sem=send_px.at[there],
            recv_sem=recv_px.at[slot],
            device_id=(there, exp),
            device_id_type=MESH,
        )

    def copy_aux(there, slot):
        return pltpu.make_async_remote_copy(
            src_ref=aux.at[there],
            dst_ref=got_aux.at[slot],
            send_sem=send_aux.at[there],
            recv_sem=recv_aux.at[slot],
            device_id=(there, exp),
            device_id_type=MESH,
        )

    def copy_reads(there, slot):
        return pltpu.make_async_remote_copy(
            src_ref=reads.at[there],
            dst_ref=got_reads.at[slot],
            send_sem=send_reads.at[there],
            recv_sem=recv_reads.at[slot],
            device_id=(there, exp),
            device_id_type=MESH,
        )

    for q, core in pairs:
        there = peer(q, core)
        copy_aux(there, me).start()
        copy_px(there, me).start()

    weights = taps[me].astype(F32)
    gain = head_gain[...]

    def features(src):
        tile = got_aux[src]
        rows = got_px[src].astype(F32)
        slot = jnp.broadcast_to(tile[:, 8:9], (S_DEV, CH))
        inputs = []
        for i in range(CONV - 1):
            window = jnp.zeros((S_DEV, CH), F32)
            for p in range(PG):
                row = jnp.broadcast_to(conv[p * 3 + i : p * 3 + i + 1, :], (S_DEV, CH))
                window = jnp.where(slot == p, row, window)
            inputs.append(window)
        for t in range(STEPS):
            inputs.append(rows[t * S_DEV : (t + 1) * S_DEV])
        queries, keys, values = [], [], []
        for t in range(STEPS):
            summed = inputs[t] * weights[0:1]
            for j in range(1, CONV):
                summed = summed + inputs[t + j] * weights[j : j + 1]
            active = swish(summed)
            q = active[:, :DK]
            k = active[:, DK : 2 * DK]
            q = q * lax.rsqrt(jnp.sum(q * q, axis=-1, keepdims=True) + EPSILON) * DK ** (-0.5)
            k = k * lax.rsqrt(jnp.sum(k * k, axis=-1, keepdims=True) + EPSILON)
            queries.append(q.astype(BF16).astype(F32))
            keys.append(k.astype(BF16).astype(F32))
            values.append(active[:, 2 * DK :].astype(BF16).astype(F32))
        return tile, queries, keys, values

    def recur(tile, queries, keys, values, projected):
        slot = jnp.broadcast_to(tile[:, 8:9], (S_DEV, DK))

        def picked(row):
            block = projected[row * S_DEV : (row + 1) * S_DEV]
            chosen = block[:, :DK]
            for p in range(1, PG):
                chosen = jnp.where(slot == p, block[:, p * DK : (p + 1) * DK], chosen)
            return chosen

        total = [tile[:, 0:1]]
        for t in range(1, STEPS):
            total.append(total[-1] + tile[:, t : t + 1])
        writes, outs = [], []
        for t in range(STEPS):
            decay = jnp.exp(total[t])
            recalled = decay * picked(STEPS + t)
            reading = decay * picked(t)
            for j in range(t):
                ratio = jnp.exp(total[t] - total[j])
                recalled = recalled + (ratio * jnp.sum(keys[j] * keys[t], axis=-1, keepdims=True)) * writes[j]
                reading = reading + (ratio * jnp.sum(keys[j] * queries[t], axis=-1, keepdims=True)) * writes[j]
            written = tile[:, STEPS + t : STEPS + t + 1] * (values[t] - recalled)
            writes.append(written)
            reading = reading + jnp.sum(keys[t] * queries[t], axis=-1, keepdims=True) * written
            mean = jnp.mean(reading * reading, axis=-1, keepdims=True)
            outs.append(reading * lax.rsqrt(mean + EPSILON) * gain)
        return jnp.concatenate(outs, axis=0).astype(BF16)

    def step(q, carry):
        first = peer(q, 0)
        second = peer(q, 1)

        @pl.when(q > 0)
        def _():
            copy_aux(first, first).wait_recv()
            copy_px(first, first).wait_recv()

        copy_aux(second, second).wait_recv()
        copy_px(second, second).wait_recv()
        parts = [features(first), features(second)]
        stacked = jnp.concatenate([v for part in parts for v in part[1] + part[2]], axis=0).astype(BF16)
        projected = jnp.dot(stacked, states[...], preferred_element_type=F32)
        for i, src in enumerate((first, second)):
            reads[pl.ds(src, 1)] = recur(*parts[i], projected[i * 64 : (i + 1) * 64])[None]

        @pl.when(q > 0)
        def _():
            copy_reads(first, me).start()

        copy_reads(second, me).start()
        return carry

    lax.fori_loop(0, RING, step, 0)
    got_reads[pl.ds(me, 1)] = reads[pl.ds(me, 1)]
    for q, core in pairs[::-1]:
        there = peer(q, core)
        copy_reads(there, there).wait_recv()

    row, col = iota((ROWS, ROWS), 0), iota((ROWS, ROWS), 1)
    order = ((row // STEPS == lax.rem(col, S_DEV)) & (lax.rem(row, STEPS) == col // S_DEV)).astype(BF16)
    squares = jnp.zeros((ROWS, 1), F32)
    for h in range(HEADS):
        lanes = slice(h * DK, (h + 1) * DK)
        normed = jnp.dot(order, got_reads[h], preferred_element_type=F32)
        value = layer_in[:, lanes].astype(F32) + normed * swish(gate_in[:, lanes].astype(F32))
        residual[:, lanes] = value
        squares = squares + jnp.sum(value * value, axis=-1, keepdims=True)
    scale = lax.rsqrt(squares / D + EPSILON)
    for half in range(2):
        lanes = slice(half * HALF, (half + 1) * HALF)
        normed_in[half] = (residual[:, lanes] * scale * post_gain[:, lanes]).astype(BF16)

    for q, core in pairs:
        there = peer(q, core)
        copy_aux(there, me).wait_send()
        copy_px(there, me).wait_send()
        copy_reads(there, me).wait_send()


def experts_kernel(
    rows_in,
    residual,
    ids,
    route,
    gate_up_hbm,
    down_hbm,
    out,
    gate_up,
    down,
    info_out,
    info_in,
    near,
    pick,
    mix_hi,
    mix_lo,
    slots_out,
    slots_in,
    hidden_sum,
    hidden,
    back_out,
    back_in,
    part_out,
    part_in,
    load_sem,
    send_sem,
    recv_sem,
):
    _, _, y, z = place()
    rep = lax.axis_index("rep")

    def along_y(o):
        return (rep, lax.rem(y + o, RING) * RING + z)

    def along_z(o):
        return (rep, y * RING + lax.rem(z + o, RING))

    first_axis, second_axis = (along_y, along_z), (along_z, along_y)

    load_gate_up = pltpu.make_async_copy(gate_up_hbm, gate_up, load_sem.at[0])
    load_down = pltpu.make_async_copy(down_hbm, down, load_sem.at[1])
    load_gate_up.start()
    load_down.start()
    barrier = pltpu.get_barrier_semaphore()
    for q in FAR_FIRST:
        for axis in (along_y, along_z):
            pl.semaphore_signal(barrier, inc=1, device_id=axis(OFFS[q]), device_id_type=MESH)

    def copy(phase, half, axis, q, src, dst):
        return pltpu.make_async_remote_copy(
            src_ref=src(q),
            dst_ref=dst(BACK[q]),
            send_sem=send_sem.at[phase * 2 + half, q],
            recv_sem=recv_sem.at[phase * 2 + half, BACK[q]],
            device_id=axis(OFFS[q]),
            device_id_type=MESH,
        )

    def blocks(ref, half, size):
        return lambda q: ref.at[half, pl.ds(q * size, size)]

    def info_copy(half, q):
        return copy(0, half, first_axis[half], q, lambda i: info_out.at[half, i], lambda i: info_in.at[half, i])

    def row_copy(half, q):
        return copy(1, half, first_axis[half], q, lambda i: rows_in.at[half], blocks(near, half, ROWS))

    def slot_copy(half, q):
        return copy(2, half, second_axis[half], q, blocks(slots_out, half, 64), blocks(slots_in, half, 64))

    def back_copy(half, q):
        return copy(3, half, second_axis[half], q, blocks(back_out, half, 64), blocks(back_in, half, 64))

    def part_copy(half, q):
        return copy(4, half, first_axis[half], q, blocks(part_out, half, ROWS), blocks(part_in, half, ROWS))

    def arrived(copy_of, half, q):
        copy_of(half, BACK[q]).wait_recv()

    def offset_of(position):
        value = jnp.zeros_like(position)
        for i, o in enumerate(OFFS):
            value = jnp.where(position == i, o, value)
        return value

    def back_of(position):
        value = jnp.zeros_like(position)
        for i, o in enumerate(BACK):
            value = jnp.where(position == i, o, value)
        return value

    shape = (64, 128)
    q_of, m_of = iota(shape, 0) // RING, lax.rem(iota(shape, 0), RING)
    lane_block = iota(shape, 1) // ROWS
    mine = lane_block == lax.rem(back_of(q_of), 4)
    near_o, far_o = offset_of(q_of), offset_of(m_of)
    for half in range(2):
        y_o, z_o = (near_o, far_o) if half == 0 else (far_o, near_o)
        expert = lax.rem(y + y_o, RING) * RING + lax.rem(z + z_o, RING)
        weight = jnp.zeros(shape, F32)
        for k in range(TOPK):
            weight = weight + jnp.where(ids[k : k + 1, :] == expert, route[k : k + 1, :], 0.0)
        weight = jnp.where(mine, weight, 0.0)
        info_out[half] = weight.reshape(RING, RING, 128)
        info_in[half, 0] = weight[:RING]
        near[half, 0:ROWS] = rows_in[half]

    pl.semaphore_wait(barrier, 2 * (RING - 1))
    for q in FAR_FIRST:
        for half in range(2):
            info_copy(half, q).start()
            row_copy(half, q).start()

    cols = RING * ROWS
    before = (
        (iota((cols, cols), 0) // ROWS == iota((cols, cols), 1) // ROWS)
        & (iota((cols, cols), 0) < iota((cols, cols), 1))
    ).astype(BF16)
    pick_rows = iota((64, cols), 0)
    diagonal = pick_rows // CAP == iota((64, cols), 1) // ROWS
    slot_of = lax.rem(pick_rows, CAP).astype(F32)
    for half in range(2):
        for q in range(1, RING):
            arrived(info_copy, half, q)
        low = info_in[half, 0] + info_in[half, 1] + info_in[half, 2] + info_in[half, 3]
        high = info_in[half, 4] + info_in[half, 5] + info_in[half, 6] + info_in[half, 7]
        weight = jnp.concatenate([low, high], axis=1)
        named = (weight > 0.0).astype(BF16)
        position = jnp.dot(named, before, preferred_element_type=F32)
        for pair in range(4):
            mixes = []
            for m in (2 * pair, 2 * pair + 1):
                w = jnp.broadcast_to(weight[m : m + 1], (64, cols))
                at = jnp.broadcast_to(position[m : m + 1], (64, cols))
                hit = diagonal & (at == slot_of) & (w > 0.0)
                pick[half, m * 64 : (m + 1) * 64] = hit.astype(F32).astype(BF16)
                mixes.append(jnp.where(hit, w, 0.0))
            mix = jnp.transpose(jnp.concatenate(mixes, axis=0))
            top = mix.astype(BF16)
            lanes = slice(pair * 128, (pair + 1) * 128)
            mix_hi[half, :, lanes] = top
            mix_lo[half, :, lanes] = (mix - top.astype(F32)).astype(BF16)

    for half in range(2):
        for q in range(1, RING):
            arrived(row_copy, half, q)
    for pair in range(3, -1, -1):
        for half in range(2):
            span = slice(pair * 128, (pair + 1) * 128)
            chosen = jnp.dot(pick[half, span], near[half], preferred_element_type=F32).astype(BF16)
            slots_out[half, span] = chosen
            if pair == 0:
                slots_in[half, 0:64] = chosen[0:64]
            for m in (2 * pair + 1, 2 * pair):
                if m:
                    slot_copy(half, m).start()

    load_gate_up.wait()
    for half in range(2):
        for m in range(1, RING):
            arrived(slot_copy, half, m)

        def up(n, carry, half=half):
            lanes = pl.ds(pl.multiple_of(n * 256, 256), 256)
            hidden_sum[half, :, lanes] = jnp.dot(
                slots_in[half], gate_up[half * HALF : (half + 1) * HALF, lanes], preferred_element_type=F32
            )
            return carry

        lax.fori_loop(0, 2 * FE // 256, up, 0)

    def activate(m, carry):
        for q in range(RING):
            here = pl.ds(pl.multiple_of(m * 64 + q * CAP, CAP), CAP)
            turned = pl.ds(pl.multiple_of(q * 64 + m * CAP, CAP), CAP)
            both = hidden_sum[0, here] + hidden_sum[1, turned]
            value = swish(both[:, :FE]) * both[:, FE:]
            hidden[0, here] = value
            hidden[1, turned] = value
        return carry

    lax.fori_loop(0, RING, activate, 0)
    load_down.wait()
    for pair in range(3, -1, -1):
        for half in range(2):
            span = slice(pair * 128, (pair + 1) * 128)
            value = jnp.dot(
                hidden[half, span].astype(BF16),
                down[:, half * HALF : (half + 1) * HALF],
                preferred_element_type=F32,
            ).astype(BF16)
            back_out[half, span] = value
            if pair == 0:
                back_in[half, 0:64] = value[0:64]
            for m in (2 * pair + 1, 2 * pair):
                if m:
                    back_copy(half, m).start()

    for half in range(2):
        for m in range(1, RING):
            arrived(back_copy, half, m)
        parts = jnp.dot(mix_hi[half], back_in[half], preferred_element_type=F32)
        parts = parts + jnp.dot(mix_lo[half], back_in[half], preferred_element_type=F32)
        part_out[half] = parts.astype(BF16)
        for q in FAR_FIRST:
            part_copy(half, q).start()
    for half in range(2):
        lanes = slice(half * HALF, (half + 1) * HALF)
        total = residual[:, lanes] + part_out[half, 0:ROWS].astype(F32)
        for q in range(1, RING):
            arrived(part_copy, half, q)
            total = total + part_in[half, q * ROWS : (q + 1) * ROWS].astype(F32)
        out[:, lanes] = total.astype(BF16)

    for half in range(2):
        for q in range(1, RING):
            for copy_of in (info_copy, row_copy, slot_copy, back_copy, part_copy):
                copy_of(half, q).wait_send()


def per_device(
    prompt_state,
    prompt_conv,
    slot_prompt,
    projected,
    conv_weight,
    log_decay,
    write_rate,
    gate_in,
    layer_in,
    head_gain,
    post_gain,
    expert_ids,
    route_weight,
    w_gate_up,
    w_down,
):
    vmem = pl.BlockSpec(memory_space=pltpu.VMEM)
    hbm = pl.BlockSpec(memory_space=pl.ANY)
    dma = pltpu.SemaphoreType.DMA

    px = jnp.transpose(projected, (2, 1, 0, 3)).reshape(HEADS, ROWS, CH)
    slots = jnp.broadcast_to(slot_prompt.astype(F32)[None, :, None], (HEADS, S_DEV, 1))
    aux = jnp.concatenate(
        [jnp.transpose(log_decay, (2, 0, 1)), jnp.transpose(write_rate, (2, 0, 1)), slots], axis=2
    )
    aux = jnp.pad(aux, ((0, 0), (0, 0), (0, 128 - aux.shape[2])))
    residual, normed_in = pl.pallas_call(
        mixer_kernel,
        out_shape=(
            jax.ShapeDtypeStruct((ROWS, D), F32),
            jax.ShapeDtypeStruct((2, ROWS, HALF), BF16),
        ),
        in_specs=[vmem] * 9,
        out_specs=(vmem, vmem),
        scratch_shapes=[
            pltpu.VMEM((HEADS, ROWS, CH), BF16),
            pltpu.VMEM((HEADS, S_DEV, 128), F32),
            pltpu.VMEM((DK, PG * DK), BF16),
            pltpu.VMEM((HEADS, ROWS, DK), BF16),
            pltpu.VMEM((HEADS, ROWS, DK), BF16),
        ]
        + [dma((HEADS,))] * 6,
        compiler_params=pltpu.CompilerParams(
            collective_id=0, has_side_effects=True, vmem_limit_bytes=VMEM_BYTES
        ),
        name="mixer",
    )(
        px,
        aux,
        prompt_state.reshape(PG, DK, DK),
        prompt_conv.reshape(PG * 3, CH).astype(F32),
        conv_weight,
        head_gain.reshape(1, DK),
        gate_in.reshape(ROWS, D),
        layer_in.reshape(ROWS, D),
        post_gain.reshape(1, D),
    )

    ids = jnp.tile(jnp.transpose(expert_ids.reshape(ROWS, TOPK)), (1, 4))
    route = jnp.tile(jnp.transpose(route_weight.reshape(ROWS, TOPK)), (1, 4))
    out = pl.pallas_call(
        experts_kernel,
        out_shape=jax.ShapeDtypeStruct((ROWS, D), BF16),
        in_specs=[vmem] * 4 + [hbm] * 2,
        out_specs=vmem,
        scratch_shapes=[
            pltpu.VMEM((D, 2 * FE), BF16),
            pltpu.VMEM((FE, D), BF16),
            pltpu.VMEM((2, RING, RING, 128), F32),
            pltpu.VMEM((2, RING, RING, 128), F32),
            pltpu.VMEM((2, RING * ROWS, HALF), BF16),
            pltpu.VMEM((2, 512, RING * ROWS), BF16),
            pltpu.VMEM((2, RING * ROWS, 512), BF16),
            pltpu.VMEM((2, RING * ROWS, 512), BF16),
            pltpu.VMEM((2, 512, HALF), BF16),
            pltpu.VMEM((2, 512, HALF), BF16),
            pltpu.VMEM((2, 512, 2 * FE), F32),
            pltpu.VMEM((2, 512, FE), F32),
            pltpu.VMEM((2, 512, HALF), BF16),
            pltpu.VMEM((2, 512, HALF), BF16),
            pltpu.VMEM((2, RING * ROWS, HALF), BF16),
            pltpu.VMEM((2, RING * ROWS, HALF), BF16),
            dma((2,)),
            dma((10, RING)),
            dma((10, RING)),
        ],
        compiler_params=pltpu.CompilerParams(
            collective_id=1, has_side_effects=True, vmem_limit_bytes=VMEM_BYTES
        ),
        name="experts",
    )(normed_in, residual, ids, route, w_gate_up.reshape(D, 2 * FE), w_down.reshape(FE, D))
    return out.reshape(layer_in.shape)


def solution(mesh):
    rows = ("rep", "exp")
    in_specs = (
        P("exp", "rep", None, None),
        P("exp", "rep", None, None),
        P(rows),
        P(rows, None, None, None),
        P(),
        P(rows, None, None),
        P(rows, None, None),
        P(rows, None, None),
        P(rows, None, None),
        P(),
        P(),
        P(rows, None, None),
        P(rows, None, None),
        P("exp", None, None),
        P("exp", None, None),
    )
    return jax.shard_map(
        per_device, mesh=mesh, in_specs=in_specs, out_specs=P(rows, None, None), check_vma=False
    )
```

```python
import jax
import jax.numpy as jnp
from jax import lax
from jax.experimental import pallas as pl
from jax.experimental.pallas import tpu as pltpu
from jax.sharding import PartitionSpec as P

MESH = pl.DeviceIdType.MESH
F32 = jnp.float32
BF16 = jnp.bfloat16

DK = 128
CH = 384
CONV = 4
FE = 512
STEPS = 4
HEADS = 16
D = 2048
HALF = 1024
PART = 512
RING = 8
S_DEV = 8
PG = 8
ROWS = 32
CAP = 8
TOPK = 10
EPSILON = 1e-06
VMEM_BYTES = 56 << 20

OFFS = (0, 1, 7, 2, 6, 3, 5, 4)
BACK = tuple(OFFS.index((RING - o) % RING) for o in OFFS)
FAR_FIRST = tuple(range(RING - 1, 0, -1))


def place():
    rep = lax.axis_index("rep")
    exp = lax.axis_index("exp")
    return rep // 2, lax.rem(rep, 2), exp // RING, lax.rem(exp, RING)


def swish(inputs):
    return inputs * jax.nn.sigmoid(inputs)


def iota(shape, dim):
    return lax.broadcasted_iota(jnp.int32, shape, dim)


def layer_kernel(
    projected_in,
    slot_prompt,
    log_decay,
    write_rate,
    state,
    conv,
    taps,
    head_gain,
    gate_in,
    layer_in,
    post_gain,
    ids,
    route,
    gate_up_hbm,
    down_hbm,
    out,
    gate_up,
    down,
    px,
    aux,
    got_px,
    got_aux,
    states,
    kept,
    reads,
    got_reads,
    gate,
    residual,
    rows_out,
    info_out,
    info_in,
    near,
    pick,
    mix_in,
    slots_out,
    slots_in,
    hidden_sum,
    hidden,
    back_out,
    back_in,
    part_out,
    part_in,
    load_sem,
    send_x,
    recv_x,
    send_sem,
    recv_sem,
):
    x, c, y, z = place()
    me = x * 2 + c
    exp = lax.axis_index("exp")

    load_gate_up = pltpu.make_async_copy(gate_up_hbm, gate_up, load_sem.at[0])
    load_down = pltpu.make_async_copy(down_hbm, down, load_sem.at[1])

    def peer(q, core):
        odd = lax.rem(q, 2)
        offset = odd * ((q + 1) // 2) + (1 - odd) * lax.rem(RING - q // 2, RING)
        return lax.rem(x + offset, RING) * 2 + lax.rem(c + core, 2)

    def along_y(o):
        return (me, lax.rem(y + o, RING) * RING + z)

    def along_z(o):
        return (me, y * RING + lax.rem(z + o, RING))

    first_axis, second_axis = (along_y, along_z), (along_z, along_y)

    pairs = [(q, core) for q in range(RING - 1, -1, -1) for core in range(2) if (q, core) != (0, 0)]
    barrier = pltpu.get_barrier_semaphore()
    for q, core in pairs:
        pl.semaphore_signal(barrier, inc=1, device_id=(peer(q, core), exp), device_id_type=MESH)
    for q in FAR_FIRST:
        for axis in (along_y, along_z):
            pl.semaphore_signal(barrier, inc=1, device_id=axis(OFFS[q]), device_id_type=MESH)
    load_gate_up.start()
    load_down.start()

    def x_copy(kind, src, dst, there, slot):
        return pltpu.make_async_remote_copy(
            src_ref=src,
            dst_ref=dst,
            send_sem=send_x.at[kind, there],
            recv_sem=recv_x.at[kind, slot],
            device_id=(there, exp),
            device_id_type=MESH,
        )

    def copy_aux(there, slot):
        return x_copy(0, aux.at[there], got_aux.at[slot], there, slot)

    def copy_px(u, there, slot):
        return x_copy(1 + u, px.at[u, there], got_px.at[u, slot], there, slot)

    def copy_reads(u, there, slot):
        return x_copy(3 + u, reads.at[u, there], got_reads.at[u, slot], there, slot)

    tile_lane = iota((S_DEV, 128), 1)
    diagonal8 = iota((S_DEV, S_DEV), 0) == iota((S_DEV, S_DEV), 1)
    slot_row = jnp.broadcast_to(slot_prompt[...].astype(F32).reshape(1, S_DEV), (S_DEV, S_DEV))
    slot_column = jnp.sum(jnp.where(diagonal8, slot_row, 0.0), axis=-1, keepdims=True)
    scalars = jnp.concatenate(
        [log_decay[:, t, :] for t in range(STEPS)] + [write_rate[:, t, :] for t in range(STEPS)], axis=1
    )
    for h in range(HEADS):
        turned = scalars if h == 0 else pltpu.roll(scalars, 128 - h, 1)
        aux[h] = jnp.where(tile_lane == 1, slot_column, turned)

    for u in range(2):
        turned = [jnp.swapaxes(projected_in[:, 2 * u + i].astype(F32), 0, 1) for i in range(2)]
        px[u] = jnp.concatenate(turned, axis=1).astype(BF16)

    pl.semaphore_wait(barrier, len(pairs) + 2 * (RING - 1))
    for q, core in pairs:
        there = peer(q, core)
        copy_aux(there, me).start()
        copy_px(0, there, me).start()

    got_aux[pl.ds(me, 1)] = aux[pl.ds(me, 1)]
    for u in range(2):
        got_px[u, pl.ds(me, 1)] = px[u, pl.ds(me, 1)]
    for p in range(PG):
        states[:, p * DK : (p + 1) * DK] = state[p]
    for t in range(STEPS):
        span = slice(t * S_DEV, (t + 1) * S_DEV)
        gate[span] = swish(gate_in[:, t, :].astype(F32))
        residual[span] = layer_in[:, t, :].astype(F32)

    def copy(phase, half, axis, q, src, dst):
        return pltpu.make_async_remote_copy(
            src_ref=src(q),
            dst_ref=dst(BACK[q]),
            send_sem=send_sem.at[phase * 2 + half, q],
            recv_sem=recv_sem.at[phase * 2 + half, BACK[q]],
            device_id=axis(OFFS[q]),
            device_id_type=MESH,
        )

    def info_copy(half, q):
        return copy(0, half, first_axis[half], q, lambda i: info_out.at[half, i], lambda i: info_in.at[half, i])

    def chunk_copy(phase, axes, out_ref, in_ref, size):
        def of_chunk(ch):
            def of(half, q):
                src = lambda i: out_ref.at[half, ch, pl.ds(i * size, size)]
                dst = lambda i: in_ref.at[half, ch, pl.ds(i * size, size)]
                return copy(phase + ch, half, axes[half], q, src, dst)

            return of

        return of_chunk

    slot_copy = chunk_copy(3, second_axis, slots_out, slots_in, 64)
    back_copy = chunk_copy(5, second_axis, back_out, back_in, 64)
    part_copy = chunk_copy(7, first_axis, part_out, part_in, ROWS)

    def row_copy(u):
        def of(half, q):
            src = lambda i: rows_out.at[half, pl.ds(u * 16, 16)]
            dst = lambda i: near.at[half, pl.ds(i * ROWS + u * 16, 16)]
            return copy(1 + u, half, first_axis[half], q, src, dst)

        return of

    def arrived(copy_of, half, q):
        copy_of(half, BACK[q]).wait_recv()

    def looked_up(table, position):
        value = jnp.zeros_like(position)
        for i, o in enumerate(table):
            value = jnp.where(position == i, o, value)
        return value

    lane = iota((1, 128), 1)
    near_o = looked_up(OFFS, lax.rem(lane // RING, RING))
    far_o = looked_up(OFFS, lax.rem(lane, RING))
    y_o = jnp.where(lane < 64, near_o, far_o)
    z_o = jnp.where(lane < 64, far_o, near_o)
    expert = lax.rem(y + y_o, RING) * RING + lax.rem(z + z_o, RING)
    named = []
    for t in range(STEPS):
        ids_t, route_t = ids[:, t, :], route[:, t, :]
        weight = jnp.zeros((S_DEV, 128), F32)
        for k in range(TOPK):
            weight = weight + jnp.where(ids_t[:, k : k + 1] == expert, route_t[:, k : k + 1], 0.0)
        named.append(weight)
    turned = jnp.transpose(jnp.concatenate(named * 4, axis=0))
    shape = (128, 128)
    mine = iota(shape, 1) // ROWS == lax.rem(looked_up(BACK, lax.rem(iota(shape, 0) // RING, RING)), 4)
    turned = jnp.where(mine, turned, 0.0)
    for half in range(2):
        weight = turned[half * 64 : (half + 1) * 64]
        info_out[half] = weight.reshape(RING, RING, 128)
        info_in[half, 0] = weight[:RING]
        for q in FAR_FIRST:
            info_copy(half, q).start()

    weights = taps[me].astype(F32)
    gain = head_gain[...]
    history = [conv[i].astype(F32) for i in range(CONV - 1)]

    def features(u, src):
        tile = got_aux[src]
        rows = [got_px[v, src].astype(F32) for v in range(u + 1)]
        rows = [part[i * S_DEV : (i + 1) * S_DEV] for part in rows for i in range(2)]
        slot = jnp.broadcast_to(tile[:, 1:2], (S_DEV, CH))
        inputs = []
        for i in range(2 * u, CONV - 1):
            window = jnp.broadcast_to(history[i][0:1], (S_DEV, CH))
            for p in range(1, PG):
                window = jnp.where(slot == p, jnp.broadcast_to(history[i][p : p + 1], (S_DEV, CH)), window)
            inputs.append(window)
        inputs = inputs + rows
        queries, keys, values = [], [], []
        for t in range(2):
            summed = inputs[t] * weights[0:1]
            for j in range(1, CONV):
                summed = summed + inputs[t + j] * weights[j : j + 1]
            active = swish(summed)
            q = active[:, :DK]
            k = active[:, DK : 2 * DK]
            q = q * lax.rsqrt(jnp.sum(q * q, axis=-1, keepdims=True) + EPSILON) * DK ** (-0.5)
            k = k * lax.rsqrt(jnp.sum(k * k, axis=-1, keepdims=True) + EPSILON)
            queries.append(q.astype(BF16).astype(F32))
            keys.append(k.astype(BF16).astype(F32))
            values.append(active[:, 2 * DK :].astype(BF16).astype(F32))
        return tile, queries, keys, values

    def recur(u, src, tile, queries, keys, values, projected):
        slot = jnp.broadcast_to(tile[:, 1:2], (S_DEV, DK))

        def picked(row):
            block = projected[row * S_DEV : (row + 1) * S_DEV]
            chosen = block[:, :DK]
            for p in range(1, PG):
                chosen = jnp.where(slot == p, block[:, p * DK : (p + 1) * DK], chosen)
            return chosen

        def column(i):
            return tile[:, i * 16 : i * 16 + 1]

        total = [column(0)]
        for t in range(1, 2 * u + 2):
            total.append(total[-1] + column(t))
        old_keys, writes = [], []
        if u:
            before = kept[src]
            old_keys, writes = [before[0], before[1]], [before[2], before[3]]
        all_keys = old_keys + keys
        outs = []
        for i in range(2):
            t = 2 * u + i
            decay = jnp.exp(total[t])
            recalled = decay * picked(2 + i)
            reading = decay * picked(i)
            for j in range(t):
                ratio = jnp.exp(total[t] - total[j])
                recalled = recalled + (ratio * jnp.sum(all_keys[j] * keys[i], axis=-1, keepdims=True)) * writes[j]
                reading = reading + (ratio * jnp.sum(all_keys[j] * queries[i], axis=-1, keepdims=True)) * writes[j]
            written = column(STEPS + t) * (values[i] - recalled)
            writes.append(written)
            reading = reading + jnp.sum(keys[i] * queries[i], axis=-1, keepdims=True) * written
            mean = jnp.mean(reading * reading, axis=-1, keepdims=True)
            outs.append(reading * lax.rsqrt(mean + EPSILON) * gain)
        if not u:
            for i, value in enumerate(keys + writes):
                kept[src, i] = value
        return jnp.concatenate(outs, axis=0).astype(BF16)

    def heads_step(u):
        def step(q, carry):
            first = peer(q, 0)
            second = peer(q, 1)

            @pl.when(q > 0)
            def _():
                if u == 0:
                    copy_aux(first, first).wait_recv()
                copy_px(u, first, first).wait_recv()

            if u == 0:
                copy_aux(second, second).wait_recv()
            copy_px(u, second, second).wait_recv()
            parts = [features(u, first), features(u, second)]
            stacked = jnp.concatenate([v for part in parts for v in part[1] + part[2]], axis=0).astype(BF16)
            projected = jnp.dot(stacked, states[...], preferred_element_type=F32)
            for i, src in enumerate((first, second)):
                reads[u, pl.ds(src, 1)] = recur(u, src, *parts[i], projected[i * 32 : (i + 1) * 32])[None]

            @pl.when(q > 0)
            def _():
                copy_reads(u, first, me).start()
                if u == 0:
                    copy_px(1, first, me).start()

            copy_reads(u, second, me).start()
            if u == 0:
                copy_px(1, second, me).start()
            return carry

        return step

    def mix(u):
        got_reads[u, pl.ds(me, 1)] = reads[u, pl.ds(me, 1)]
        for q, core in pairs[::-1]:
            there = peer(q, core)
            copy_reads(u, there, there).wait_recv()
        span = slice(u * 16, (u + 1) * 16)
        squares = jnp.zeros((16, 128), F32)
        for h in range(HEADS):
            lanes = slice(h * DK, (h + 1) * DK)
            value = residual[span, lanes] + got_reads[u, h].astype(F32) * gate[span, lanes]
            residual[span, lanes] = value
            squares = squares + value * value
        scale = lax.rsqrt(jnp.sum(squares, axis=-1, keepdims=True) / D + EPSILON)
        for half in range(2):
            lanes = slice(half * HALF, (half + 1) * HALF)
            value = (residual[span, lanes] * scale * post_gain[:, lanes]).astype(BF16)
            rows_out[half, span] = value
            near[half, span] = value
        for q in FAR_FIRST:
            for half in range(2):
                row_copy(u)(half, q).start()

    lax.fori_loop(0, RING, heads_step(0), 0)
    lax.fori_loop(0, RING // 2, heads_step(1), 0)
    mix(0)
    lax.fori_loop(RING // 2, RING, heads_step(1), 0)

    cols = RING * ROWS
    earlier = (
        (iota((cols, cols), 0) // ROWS == iota((cols, cols), 1) // ROWS)
        & (iota((cols, cols), 0) < iota((cols, cols), 1))
    ).astype(BF16)
    pick_rows = iota((64, cols), 0)
    diagonal = pick_rows // CAP == iota((64, cols), 1) // ROWS
    slot_of = lax.rem(pick_rows, CAP).astype(F32)
    route_in = []
    for half in range(2):
        for q in range(1, RING):
            arrived(info_copy, half, q)
        low = info_in[half, 0] + info_in[half, 1] + info_in[half, 2] + info_in[half, 3]
        high = info_in[half, 4] + info_in[half, 5] + info_in[half, 6] + info_in[half, 7]
        weight = jnp.concatenate([low, high], axis=1)
        position = jnp.dot((weight > 0.0).astype(BF16), earlier, preferred_element_type=F32)
        route_in.append((weight, position))

    def hits(half, m):
        weight, position = route_in[half]
        w = jnp.broadcast_to(weight[m : m + 1], (64, cols))
        at = jnp.broadcast_to(position[m : m + 1], (64, cols))
        return diagonal & (at == slot_of) & (w > 0.0), w

    mix(1)
    for half in range(2):
        for m in range(RING):
            pick[half, m * 64 : (m + 1) * 64] = hits(half, m)[0].astype(F32).astype(BF16)

    for half in range(2):
        for q in range(1, RING):
            arrived(row_copy(0), half, q)
            arrived(row_copy(1), half, q)
    for ch in range(2):
        lanes = slice(ch * PART, (ch + 1) * PART)
        for half in range(2):
            chosen = jnp.dot(pick[half], near[half, :, lanes], preferred_element_type=F32).astype(BF16)
            slots_out[half, ch] = chosen
            slots_in[half, ch, 0:64] = chosen[0:64]
            for m in FAR_FIRST:
                slot_copy(ch)(half, m).start()

    for half in range(2):
        for pair in range(4):
            mixes = []
            for m in (2 * pair, 2 * pair + 1):
                hit, w = hits(half, m)
                mixes.append(jnp.where(hit, w, 0.0))
            turned = jnp.transpose(jnp.concatenate(mixes, axis=0))
            mix_in[half, :, pair * 128 : (pair + 1) * 128] = turned.astype(BF16)

    load_gate_up.wait()
    for ch in range(2):
        for half in range(2):
            for m in range(1, RING):
                arrived(slot_copy(ch), half, m)

            def up(n, carry, half=half, ch=ch):
                lanes = pl.ds(pl.multiple_of(n * 256, 256), 256)
                depth = slice(half * HALF + ch * PART, half * HALF + (ch + 1) * PART)
                product = jnp.dot(slots_in[half, ch], gate_up[depth, lanes], preferred_element_type=F32)
                if ch:
                    product = product + hidden_sum[half, :, lanes]
                hidden_sum[half, :, lanes] = product
                return carry

            lax.fori_loop(0, 2 * FE // 256, up, 0)

    def activate(m, carry):
        for q in range(RING):
            here = pl.ds(pl.multiple_of(m * 64 + q * CAP, CAP), CAP)
            turned = pl.ds(pl.multiple_of(q * 64 + m * CAP, CAP), CAP)
            both = hidden_sum[0, here] + hidden_sum[1, turned]
            value = swish(both[:, :FE]) * both[:, FE:]
            hidden[0, here] = value
            hidden[1, turned] = value
        return carry

    lax.fori_loop(0, RING, activate, 0)
    load_down.wait()
    for ch in range(2):
        for half in range(2):
            lanes = slice(half * HALF + ch * PART, half * HALF + (ch + 1) * PART)
            value = jnp.dot(hidden[half].astype(BF16), down[:, lanes], preferred_element_type=F32).astype(BF16)
            back_out[half, ch] = value
            back_in[half, ch, 0:64] = value[0:64]
            for m in FAR_FIRST:
                back_copy(ch)(half, m).start()

    for ch in range(2):
        for half in range(2):
            for m in range(1, RING):
                arrived(back_copy(ch), half, m)
            parts = jnp.dot(mix_in[half], back_in[half, ch], preferred_element_type=F32)
            part_out[half, ch] = parts.astype(BF16)
            for q in FAR_FIRST:
                part_copy(ch)(half, q).start()
    for ch in range(2):
        for half in range(2):
            lanes = slice(half * HALF + ch * PART, half * HALF + (ch + 1) * PART)
            total = residual[:, lanes] + part_out[half, ch, 0:ROWS].astype(F32)
            for q in range(1, RING):
                arrived(part_copy(ch), half, q)
                total = total + part_in[half, ch, q * ROWS : (q + 1) * ROWS].astype(F32)
            for t in range(STEPS):
                out[:, t, lanes] = total[t * S_DEV : (t + 1) * S_DEV].astype(BF16)

    for half in range(2):
        for q in range(1, RING):
            info_copy(half, q).wait_send()
            for i in range(2):
                for copy_of in (row_copy, slot_copy, back_copy, part_copy):
                    copy_of(i)(half, q).wait_send()
    for q, core in pairs:
        there = peer(q, core)
        copy_aux(there, me).wait_send()
        for u in range(2):
            copy_px(u, there, me).wait_send()
            copy_reads(u, there, me).wait_send()


def per_device(
    prompt_state,
    prompt_conv,
    slot_prompt,
    projected,
    conv_weight,
    log_decay,
    write_rate,
    gate_in,
    layer_in,
    head_gain,
    post_gain,
    expert_ids,
    route_weight,
    w_gate_up,
    w_down,
):
    vmem = pl.BlockSpec(memory_space=pltpu.VMEM)
    hbm = pl.BlockSpec(memory_space=pl.ANY)
    dma = pltpu.SemaphoreType.DMA

    return pl.pallas_call(
        layer_kernel,
        out_shape=jax.ShapeDtypeStruct(layer_in.shape, BF16),
        in_specs=[vmem] * 13 + [hbm] * 2,
        out_specs=vmem,
        scratch_shapes=[
            pltpu.VMEM((D, 2 * FE), BF16),
            pltpu.VMEM((FE, D), BF16),
            pltpu.VMEM((2, HEADS, 16, CH), BF16),
            pltpu.VMEM((HEADS, S_DEV, 128), F32),
            pltpu.VMEM((2, HEADS, 16, CH), BF16),
            pltpu.VMEM((HEADS, S_DEV, 128), F32),
            pltpu.VMEM((DK, PG * DK), BF16),
            pltpu.VMEM((HEADS, 4, S_DEV, DK), F32),
            pltpu.VMEM((2, HEADS, 16, DK), BF16),
            pltpu.VMEM((2, HEADS, 16, DK), BF16),
            pltpu.VMEM((ROWS, D), F32),
            pltpu.VMEM((ROWS, D), F32),
            pltpu.VMEM((2, ROWS, HALF), BF16),
            pltpu.VMEM((2, RING, RING, 128), F32),
            pltpu.VMEM((2, RING, RING, 128), F32),
            pltpu.VMEM((2, RING * ROWS, HALF), BF16),
            pltpu.VMEM((2, 512, RING * ROWS), BF16),
            pltpu.VMEM((2, RING * ROWS, 512), BF16),
            pltpu.VMEM((2, 2, 512, PART), BF16),
            pltpu.VMEM((2, 2, 512, PART), BF16),
            pltpu.VMEM((2, 512, 2 * FE), F32),
            pltpu.VMEM((2, 512, FE), F32),
            pltpu.VMEM((2, 2, 512, PART), BF16),
            pltpu.VMEM((2, 2, 512, PART), BF16),
            pltpu.VMEM((2, 2, RING * ROWS, PART), BF16),
            pltpu.VMEM((2, 2, RING * ROWS, PART), BF16),
            dma((2,)),
            dma((5, HEADS)),
            dma((5, HEADS)),
            dma((18, RING)),
            dma((18, RING)),
        ],
        compiler_params=pltpu.CompilerParams(
            collective_id=0, has_side_effects=True, vmem_limit_bytes=VMEM_BYTES
        ),
        name="layer",
    )(
        projected,
        slot_prompt,
        log_decay,
        write_rate,
        prompt_state.reshape(PG, DK, DK),
        jnp.transpose(prompt_conv, (1, 2, 0, 3)).reshape(CONV - 1, PG, CH),
        conv_weight,
        head_gain.reshape(1, DK),
        gate_in,
        layer_in,
        post_gain.reshape(1, D),
        expert_ids,
        route_weight,
        w_gate_up.reshape(D, 2 * FE),
        w_down.reshape(FE, D),
    )


def solution(mesh):
    rows = ("rep", "exp")
    in_specs = (
        P("exp", "rep", None, None),
        P("exp", "rep", None, None),
        P(rows),
        P(rows, None, None, None),
        P(),
        P(rows, None, None),
        P(rows, None, None),
        P(rows, None, None),
        P(rows, None, None),
        P(),
        P(),
        P(rows, None, None),
        P(rows, None, None),
        P("exp", None, None),
        P("exp", None, None),
    )
    return jax.shard_map(
        per_device, mesh=mesh, in_specs=in_specs, out_specs=P(rows, None, None), check_vma=False
    )
```

```python
import jax
import jax.numpy as jnp
from jax import lax
from jax.experimental import pallas as pl
from jax.experimental.pallas import tpu as pltpu
from jax.sharding import PartitionSpec as P

MESH = pl.DeviceIdType.MESH
F32 = jnp.float32
BF16 = jnp.bfloat16

DK = 128
CH = 384
CONV = 4
FE = 512
STEPS = 4
HEADS = 16
D = 2048
HALF = 1024
PART = 512
RING = 8
S_DEV = 8
PG = 8
ROWS = 32
CAP = 8
TOPK = 10
EPSILON = 1e-06
VMEM_BYTES = 56 << 20

OFFS = (0, 1, 7, 2, 6, 3, 5, 4)
BACK = tuple(OFFS.index((RING - o) % RING) for o in OFFS)
FAR_FIRST = tuple(range(RING - 1, 0, -1))


def place():
    rep = lax.axis_index("rep")
    exp = lax.axis_index("exp")
    return rep // 2, lax.rem(rep, 2), exp // RING, lax.rem(exp, RING)


def swish(inputs):
    return inputs * jax.nn.sigmoid(inputs)


def iota(shape, dim):
    return lax.broadcasted_iota(jnp.int32, shape, dim)


def layer_kernel(
    projected_in,
    slot_prompt,
    log_decay,
    write_rate,
    state_hbm,
    conv,
    taps,
    head_gain,
    gate_hbm,
    layer_hbm,
    post_gain,
    ids,
    route,
    gate_up_hbm,
    down_hbm,
    out,
    gate_up,
    down,
    state,
    gate_in,
    layer_in,
    px,
    aux,
    got_px,
    got_aux,
    states,
    kept,
    reads,
    got_reads,
    gate,
    residual,
    rows_out,
    info_out,
    info_in,
    near,
    pick,
    mix_in,
    slots_out,
    slots_in,
    hidden_sum,
    hidden,
    back_out,
    back_in,
    part_out,
    part_in,
    load_sem,
    send_x,
    recv_x,
    send_sem,
    recv_sem,
):
    x, c, y, z = place()
    me = x * 2 + c
    exp = lax.axis_index("exp")

    load_gate_up = pltpu.make_async_copy(gate_up_hbm, gate_up, load_sem.at[0])
    load_down = pltpu.make_async_copy(down_hbm, down, load_sem.at[1])
    load_inputs = [
        pltpu.make_async_copy(src, dst, load_sem.at[2 + i])
        for i, (src, dst) in enumerate(((state_hbm, state), (gate_hbm, gate_in), (layer_hbm, layer_in)))
    ]

    def peer(q, core):
        odd = lax.rem(q, 2)
        offset = odd * ((q + 1) // 2) + (1 - odd) * lax.rem(RING - q // 2, RING)
        return lax.rem(x + offset, RING) * 2 + lax.rem(c + core, 2)

    def along_y(o):
        return (me, lax.rem(y + o, RING) * RING + z)

    def along_z(o):
        return (me, y * RING + lax.rem(z + o, RING))

    first_axis, second_axis = (along_y, along_z), (along_z, along_y)

    pairs = [(q, core) for q in range(RING - 1, -1, -1) for core in range(2) if (q, core) != (0, 0)]
    barrier = pltpu.get_barrier_semaphore()
    for q, core in pairs:
        pl.semaphore_signal(barrier, inc=1, device_id=(peer(q, core), exp), device_id_type=MESH)
    for q in FAR_FIRST:
        for axis in (along_y, along_z):
            pl.semaphore_signal(barrier, inc=1, device_id=axis(OFFS[q]), device_id_type=MESH)
    for load in load_inputs:
        load.start()
    load_gate_up.start()
    load_down.start()

    def x_copy(kind, src, dst, there, slot):
        return pltpu.make_async_remote_copy(
            src_ref=src,
            dst_ref=dst,
            send_sem=send_x.at[kind, there],
            recv_sem=recv_x.at[kind, slot],
            device_id=(there, exp),
            device_id_type=MESH,
        )

    def copy_aux(there, slot):
        return x_copy(0, aux.at[there], got_aux.at[slot], there, slot)

    def copy_px(u, there, slot):
        return x_copy(1 + u, px.at[u, there], got_px.at[u, slot], there, slot)

    def copy_reads(u, there, slot):
        return x_copy(3 + u, reads.at[u, there], got_reads.at[u, slot], there, slot)

    tile_lane = iota((S_DEV, 128), 1)
    diagonal8 = iota((S_DEV, S_DEV), 0) == iota((S_DEV, S_DEV), 1)
    slot_row = jnp.broadcast_to(slot_prompt[...].astype(F32).reshape(1, S_DEV), (S_DEV, S_DEV))
    slot_column = jnp.sum(jnp.where(diagonal8, slot_row, 0.0), axis=-1, keepdims=True)
    scalars = jnp.concatenate(
        [log_decay[:, t, :] for t in range(STEPS)] + [write_rate[:, t, :] for t in range(STEPS)], axis=1
    )
    for h in range(HEADS):
        turned = scalars if h == 0 else pltpu.roll(scalars, 128 - h, 1)
        aux[h] = jnp.where(tile_lane == 1, slot_column, turned)

    def lay_out(u):
        turned = [jnp.swapaxes(projected_in[:, 2 * u + i].astype(F32), 0, 1) for i in range(2)]
        px[u] = jnp.concatenate(turned, axis=1).astype(BF16)

    lay_out(0)
    pl.semaphore_wait(barrier, len(pairs) + 2 * (RING - 1))
    for q, core in pairs:
        there = peer(q, core)
        copy_aux(there, me).start()
        copy_px(0, there, me).start()

    lay_out(1)
    got_aux[pl.ds(me, 1)] = aux[pl.ds(me, 1)]
    for u in range(2):
        got_px[u, pl.ds(me, 1)] = px[u, pl.ds(me, 1)]
    for load in load_inputs:
        load.wait()
    for p in range(PG):
        states[:, p * DK : (p + 1) * DK] = state[p]
    for t in range(STEPS):
        span = slice(t * S_DEV, (t + 1) * S_DEV)
        gate[span] = swish(gate_in[:, t, :].astype(F32))
        residual[span] = layer_in[:, t, :].astype(F32)

    def copy(phase, half, axis, q, src, dst):
        return pltpu.make_async_remote_copy(
            src_ref=src(q),
            dst_ref=dst(BACK[q]),
            send_sem=send_sem.at[phase * 2 + half, q],
            recv_sem=recv_sem.at[phase * 2 + half, BACK[q]],
            device_id=axis(OFFS[q]),
            device_id_type=MESH,
        )

    def info_copy(half, q):
        return copy(0, half, first_axis[half], q, lambda i: info_out.at[half, i], lambda i: info_in.at[half, i])

    def chunk_copy(phase, axes, out_ref, in_ref, size):
        def of_chunk(ch):
            def of(half, q):
                src = lambda i: out_ref.at[half, ch, pl.ds(i * size, size)]
                dst = lambda i: in_ref.at[half, ch, pl.ds(i * size, size)]
                return copy(phase + ch, half, axes[half], q, src, dst)

            return of

        return of_chunk

    slot_copy = chunk_copy(3, second_axis, slots_out, slots_in, 64)
    back_copy = chunk_copy(5, second_axis, back_out, back_in, 64)
    part_copy = chunk_copy(7, first_axis, part_out, part_in, ROWS)

    def row_copy(u):
        def of(half, q):
            src = lambda i: rows_out.at[half, pl.ds(u * 16, 16)]
            dst = lambda i: near.at[half, pl.ds(i * ROWS + u * 16, 16)]
            return copy(1 + u, half, first_axis[half], q, src, dst)

        return of

    def arrived(copy_of, half, q):
        copy_of(half, BACK[q]).wait_recv()

    def looked_up(table, position):
        value = jnp.zeros_like(position)
        for i, o in enumerate(table):
            value = jnp.where(position == i, o, value)
        return value

    lane = iota((1, 128), 1)
    near_o = looked_up(OFFS, lax.rem(lane // RING, RING))
    far_o = looked_up(OFFS, lax.rem(lane, RING))
    y_o = jnp.where(lane < 64, near_o, far_o)
    z_o = jnp.where(lane < 64, far_o, near_o)
    expert = lax.rem(y + y_o, RING) * RING + lax.rem(z + z_o, RING)
    named = []
    for t in range(STEPS):
        ids_t, route_t = ids[:, t, :], route[:, t, :]
        weight = jnp.zeros((S_DEV, 128), F32)
        for k in range(TOPK):
            weight = weight + jnp.where(ids_t[:, k : k + 1] == expert, route_t[:, k : k + 1], 0.0)
        named.append(weight)
    turned = jnp.transpose(jnp.concatenate(named * 4, axis=0))
    shape = (128, 128)
    mine = iota(shape, 1) // ROWS == lax.rem(looked_up(BACK, lax.rem(iota(shape, 0) // RING, RING)), 4)
    turned = jnp.where(mine, turned, 0.0)
    for half in range(2):
        weight = turned[half * 64 : (half + 1) * 64]
        info_out[half] = weight.reshape(RING, RING, 128)
        info_in[half, 0] = weight[:RING]
        for q in FAR_FIRST:
            info_copy(half, q).start()

    weights = taps[me].astype(F32)
    gain = head_gain[...]
    history = [conv[i].astype(F32) for i in range(CONV - 1)]

    def features(u, src):
        tile = got_aux[src]
        rows = [got_px[v, src].astype(F32) for v in range(u + 1)]
        rows = [part[i * S_DEV : (i + 1) * S_DEV] for part in rows for i in range(2)]
        slot = jnp.broadcast_to(tile[:, 1:2], (S_DEV, CH))
        inputs = []
        for i in range(2 * u, CONV - 1):
            window = jnp.broadcast_to(history[i][0:1], (S_DEV, CH))
            for p in range(1, PG):
                window = jnp.where(slot == p, jnp.broadcast_to(history[i][p : p + 1], (S_DEV, CH)), window)
            inputs.append(window)
        inputs = inputs + rows
        queries, keys, values = [], [], []
        for t in range(2):
            summed = inputs[t] * weights[0:1]
            for j in range(1, CONV):
                summed = summed + inputs[t + j] * weights[j : j + 1]
            active = swish(summed)
            q = active[:, :DK]
            k = active[:, DK : 2 * DK]
            q = q * lax.rsqrt(jnp.sum(q * q, axis=-1, keepdims=True) + EPSILON) * DK ** (-0.5)
            k = k * lax.rsqrt(jnp.sum(k * k, axis=-1, keepdims=True) + EPSILON)
            queries.append(q.astype(BF16).astype(F32))
            keys.append(k.astype(BF16).astype(F32))
            values.append(active[:, 2 * DK :].astype(BF16).astype(F32))
        return tile, queries, keys, values

    def recur(u, src, tile, queries, keys, values, projected):
        slot = jnp.broadcast_to(tile[:, 1:2], (S_DEV, DK))

        def picked(row):
            block = projected[row * S_DEV : (row + 1) * S_DEV]
            chosen = block[:, :DK]
            for p in range(1, PG):
                chosen = jnp.where(slot == p, block[:, p * DK : (p + 1) * DK], chosen)
            return chosen

        def column(i):
            return tile[:, i * 16 : i * 16 + 1]

        total = [column(0)]
        for t in range(1, 2 * u + 2):
            total.append(total[-1] + column(t))
        old_keys, writes = [], []
        if u:
            before = kept[src]
            old_keys, writes = [before[0], before[1]], [before[2], before[3]]
        all_keys = old_keys + keys
        outs = []
        for i in range(2):
            t = 2 * u + i
            decay = jnp.exp(total[t])
            recalled = decay * picked(2 + i)
            reading = decay * picked(i)
            for j in range(t):
                ratio = jnp.exp(total[t] - total[j])
                recalled = recalled + (ratio * jnp.sum(all_keys[j] * keys[i], axis=-1, keepdims=True)) * writes[j]
                reading = reading + (ratio * jnp.sum(all_keys[j] * queries[i], axis=-1, keepdims=True)) * writes[j]
            written = column(STEPS + t) * (values[i] - recalled)
            writes.append(written)
            reading = reading + jnp.sum(keys[i] * queries[i], axis=-1, keepdims=True) * written
            mean = jnp.mean(reading * reading, axis=-1, keepdims=True)
            outs.append(reading * lax.rsqrt(mean + EPSILON) * gain)
        if not u:
            for i, value in enumerate(keys + writes):
                kept[src, i] = value
        return jnp.concatenate(outs, axis=0).astype(BF16)

    def heads_step(u, count):
        def step(i, carry):
            at = [(RING - 1 - i * count - j, core) for j in range(count) for core in range(2)]
            sources = [peer(q, core) for q, core in at]

            def each_other(act):
                for (q, core), src in zip(at, sources):
                    if core:
                        act(src)
                    else:

                        @pl.when(q > 0)
                        def _(src=src):
                            act(src)

            def wait(src):
                if u == 0:
                    copy_aux(src, src).wait_recv()
                copy_px(u, src, src).wait_recv()

            def send(src):
                copy_reads(u, src, me).start()

            each_other(wait)
            if u == 0:
                each_other(lambda src: copy_px(1, src, me).start())
            parts = [features(u, src) for src in sources]
            stacked = jnp.concatenate([v for part in parts for v in part[1] + part[2]], axis=0).astype(BF16)
            projected = jnp.dot(stacked, states[...], preferred_element_type=F32)
            for k, src in enumerate(sources):
                reads[u, pl.ds(src, 1)] = recur(u, src, *parts[k], projected[k * 32 : (k + 1) * 32])[None]
            each_other(send)
            return carry

        return step

    def mix(u):
        got_reads[u, pl.ds(me, 1)] = reads[u, pl.ds(me, 1)]
        for q, core in pairs[::-1]:
            there = peer(q, core)
            copy_reads(u, there, there).wait_recv()
        span = slice(u * 16, (u + 1) * 16)
        squares = jnp.zeros((16, 128), F32)
        for h in range(HEADS):
            lanes = slice(h * DK, (h + 1) * DK)
            value = residual[span, lanes] + got_reads[u, h].astype(F32) * gate[span, lanes]
            residual[span, lanes] = value
            squares = squares + value * value
        scale = lax.rsqrt(jnp.sum(squares, axis=-1, keepdims=True) / D + EPSILON)
        for half in range(2):
            lanes = slice(half * HALF, (half + 1) * HALF)
            value = (residual[span, lanes] * scale * post_gain[:, lanes]).astype(BF16)
            rows_out[half, span] = value
            near[half, span] = value
        for q in FAR_FIRST:
            for half in range(2):
                row_copy(u)(half, q).start()

    lax.fori_loop(0, RING // 2, heads_step(0, 2), 0)
    lax.fori_loop(0, RING // 4, heads_step(1, 2), 0)
    mix(0)
    lax.fori_loop(RING // 4, RING // 2, heads_step(1, 2), 0)

    cols = RING * ROWS
    earlier = (
        (iota((cols, cols), 0) // ROWS == iota((cols, cols), 1) // ROWS)
        & (iota((cols, cols), 0) < iota((cols, cols), 1))
    ).astype(BF16)
    pick_rows = iota((64, cols), 0)
    diagonal = pick_rows // CAP == iota((64, cols), 1) // ROWS
    slot_of = lax.rem(pick_rows, CAP).astype(F32)
    route_in = []
    for half in range(2):
        for q in range(1, RING):
            arrived(info_copy, half, q)
        low = info_in[half, 0] + info_in[half, 1] + info_in[half, 2] + info_in[half, 3]
        high = info_in[half, 4] + info_in[half, 5] + info_in[half, 6] + info_in[half, 7]
        weight = jnp.concatenate([low, high], axis=1)
        position = jnp.dot((weight > 0.0).astype(BF16), earlier, preferred_element_type=F32)
        route_in.append((weight, position))

    def hits(half, m):
        weight, position = route_in[half]
        w = jnp.broadcast_to(weight[m : m + 1], (64, cols))
        at = jnp.broadcast_to(position[m : m + 1], (64, cols))
        return diagonal & (at == slot_of) & (w > 0.0), w

    mix(1)
    for half in range(2):
        for m in range(RING):
            pick[half, m * 64 : (m + 1) * 64] = hits(half, m)[0].astype(F32).astype(BF16)

    for half in range(2):
        for q in range(1, RING):
            arrived(row_copy(0), half, q)
            arrived(row_copy(1), half, q)
    for ch in range(2):
        lanes = slice(ch * PART, (ch + 1) * PART)
        for half in range(2):
            chosen = jnp.dot(pick[half], near[half, :, lanes], preferred_element_type=F32).astype(BF16)
            slots_out[half, ch] = chosen
            slots_in[half, ch, 0:64] = chosen[0:64]
            for m in FAR_FIRST:
                slot_copy(ch)(half, m).start()

    for half in range(2):
        for pair in range(4):
            mixes = []
            for m in (2 * pair, 2 * pair + 1):
                hit, w = hits(half, m)
                mixes.append(jnp.where(hit, w, 0.0))
            turned = jnp.transpose(jnp.concatenate(mixes, axis=0))
            mix_in[half, :, pair * 128 : (pair + 1) * 128] = turned.astype(BF16)

    load_gate_up.wait()
    for ch in range(2):
        for half in range(2):
            for m in range(1, RING):
                arrived(slot_copy(ch), half, m)

            def up(n, carry, half=half, ch=ch):
                lanes = pl.ds(pl.multiple_of(n * 256, 256), 256)
                depth = slice(half * HALF + ch * PART, half * HALF + (ch + 1) * PART)
                product = jnp.dot(slots_in[half, ch], gate_up[depth, lanes], preferred_element_type=F32)
                if ch:
                    product = product + hidden_sum[half, :, lanes]
                hidden_sum[half, :, lanes] = product
                return carry

            lax.fori_loop(0, 2 * FE // 256, up, 0)

    def activate(m, carry):
        for q in range(RING):
            here = pl.ds(pl.multiple_of(m * 64 + q * CAP, CAP), CAP)
            turned = pl.ds(pl.multiple_of(q * 64 + m * CAP, CAP), CAP)
            both = hidden_sum[0, here] + hidden_sum[1, turned]
            value = swish(both[:, :FE]) * both[:, FE:]
            hidden[0, here] = value
            hidden[1, turned] = value
        return carry

    lax.fori_loop(0, RING, activate, 0)
    load_down.wait()
    for ch in range(2):
        for half in range(2):
            lanes = slice(half * HALF + ch * PART, half * HALF + (ch + 1) * PART)
            value = jnp.dot(hidden[half].astype(BF16), down[:, lanes], preferred_element_type=F32).astype(BF16)
            back_out[half, ch] = value
            back_in[half, ch, 0:64] = value[0:64]
            for m in FAR_FIRST:
                back_copy(ch)(half, m).start()

    for ch in range(2):
        for half in range(2):
            for m in range(1, RING):
                arrived(back_copy(ch), half, m)
            parts = jnp.dot(mix_in[half], back_in[half, ch], preferred_element_type=F32)
            part_out[half, ch] = parts.astype(BF16)
            for q in FAR_FIRST:
                part_copy(ch)(half, q).start()
    for ch in range(2):
        for half in range(2):
            lanes = slice(half * HALF + ch * PART, half * HALF + (ch + 1) * PART)
            total = residual[:, lanes] + part_out[half, ch, 0:ROWS].astype(F32)
            for q in range(1, RING):
                arrived(part_copy(ch), half, q)
                total = total + part_in[half, ch, q * ROWS : (q + 1) * ROWS].astype(F32)
            for t in range(STEPS):
                out[:, t, lanes] = total[t * S_DEV : (t + 1) * S_DEV].astype(BF16)

    for half in range(2):
        for q in range(1, RING):
            info_copy(half, q).wait_send()
            for i in range(2):
                for copy_of in (row_copy, slot_copy, back_copy, part_copy):
                    copy_of(i)(half, q).wait_send()
    for q, core in pairs:
        there = peer(q, core)
        copy_aux(there, me).wait_send()
        for u in range(2):
            copy_px(u, there, me).wait_send()
            copy_reads(u, there, me).wait_send()


def per_device(
    prompt_state,
    prompt_conv,
    slot_prompt,
    projected,
    conv_weight,
    log_decay,
    write_rate,
    gate_in,
    layer_in,
    head_gain,
    post_gain,
    expert_ids,
    route_weight,
    w_gate_up,
    w_down,
):
    vmem = pl.BlockSpec(memory_space=pltpu.VMEM)
    hbm = pl.BlockSpec(memory_space=pl.ANY)
    dma = pltpu.SemaphoreType.DMA

    return pl.pallas_call(
        layer_kernel,
        out_shape=jax.ShapeDtypeStruct(layer_in.shape, BF16),
        in_specs=[vmem] * 4 + [hbm] + [vmem] * 3 + [hbm] * 2 + [vmem] * 3 + [hbm] * 2,
        out_specs=vmem,
        scratch_shapes=[
            pltpu.VMEM((D, 2 * FE), BF16),
            pltpu.VMEM((FE, D), BF16),
            pltpu.VMEM((PG, DK, DK), BF16),
            pltpu.VMEM((S_DEV, STEPS, D), BF16),
            pltpu.VMEM((S_DEV, STEPS, D), BF16),
            pltpu.VMEM((2, HEADS, 16, CH), BF16),
            pltpu.VMEM((HEADS, S_DEV, 128), F32),
            pltpu.VMEM((2, HEADS, 16, CH), BF16),
            pltpu.VMEM((HEADS, S_DEV, 128), F32),
            pltpu.VMEM((DK, PG * DK), BF16),
            pltpu.VMEM((HEADS, 4, S_DEV, DK), F32),
            pltpu.VMEM((2, HEADS, 16, DK), BF16),
            pltpu.VMEM((2, HEADS, 16, DK), BF16),
            pltpu.VMEM((ROWS, D), F32),
            pltpu.VMEM((ROWS, D), F32),
            pltpu.VMEM((2, ROWS, HALF), BF16),
            pltpu.VMEM((2, RING, RING, 128), F32),
            pltpu.VMEM((2, RING, RING, 128), F32),
            pltpu.VMEM((2, RING * ROWS, HALF), BF16),
            pltpu.VMEM((2, 512, RING * ROWS), BF16),
            pltpu.VMEM((2, RING * ROWS, 512), BF16),
            pltpu.VMEM((2, 2, 512, PART), BF16),
            pltpu.VMEM((2, 2, 512, PART), BF16),
            pltpu.VMEM((2, 512, 2 * FE), F32),
            pltpu.VMEM((2, 512, FE), F32),
            pltpu.VMEM((2, 2, 512, PART), BF16),
            pltpu.VMEM((2, 2, 512, PART), BF16),
            pltpu.VMEM((2, 2, RING * ROWS, PART), BF16),
            pltpu.VMEM((2, 2, RING * ROWS, PART), BF16),
            dma((5,)),
            dma((5, HEADS)),
            dma((5, HEADS)),
            dma((18, RING)),
            dma((18, RING)),
        ],
        compiler_params=pltpu.CompilerParams(
            collective_id=0, has_side_effects=True, vmem_limit_bytes=VMEM_BYTES
        ),
        name="layer",
    )(
        projected,
        slot_prompt,
        log_decay,
        write_rate,
        prompt_state.reshape(PG, DK, DK),
        jnp.transpose(prompt_conv, (1, 2, 0, 3)).reshape(CONV - 1, PG, CH),
        conv_weight,
        head_gain.reshape(1, DK),
        gate_in,
        layer_in,
        post_gain.reshape(1, D),
        expert_ids,
        route_weight,
        w_gate_up.reshape(D, 2 * FE),
        w_down.reshape(FE, D),
    )


def solution(mesh):
    rows = ("rep", "exp")
    in_specs = (
        P("exp", "rep", None, None),
        P("exp", "rep", None, None),
        P(rows),
        P(rows, None, None, None),
        P(),
        P(rows, None, None),
        P(rows, None, None),
        P(rows, None, None),
        P(rows, None, None),
        P(),
        P(),
        P(rows, None, None),
        P(rows, None, None),
        P("exp", None, None),
        P("exp", None, None),
    )
    return jax.shard_map(
        per_device, mesh=mesh, in_specs=in_specs, out_specs=P(rows, None, None), check_vma=False
    )
```
